32 devices in a mesh: wide: 16 (over z, y, x), narrow: 2 (over core).
Axes of the slice: x: 2, y: 2, z: 4, core: 2. Of those that a mesh axis runs over, the one named last changes fastest.
Arguments:
- queries: bfloat16 [4096, 2048], P(('wide', 'narrow')), may hold values from -6 to 6
- keys: bfloat16 [4096, 2048], P(('wide', 'narrow')), may hold values from -6 to 6
- values: bfloat16 [4096, 2048], P(('wide', 'narrow')), may hold values from -6 to 6
Outputs:
- attended: bfloat16 [4096, 2048], P(('wide', 'narrow'))
The draws below stay inside these ranges and needn't reach their ends.
All inputs are finite; a program needn't handle non-finite values.
Results may differ from the reference program's by a relative error of at most 0.008.
Values sent between devices are 32-bit elements; how exact they have to be, the bound alone decides.
No kernel may reach another device: no remote copies, remote signals or barrier semaphores. Data moves between devices by JAX's collectives and lax.ppermute only.
A program may use at most 192 MiB of HBM per device.

```python
import jax
import jax.numpy as jnp
from jax import lax

HEADS = 16
HEAD_DIM = 128
TOK_DEV = 128
SEQ = 4096
WIDTH = 2048


def steps_of(own_key, extent, split, low, top_value):
    gain, own = 1.0, jax.random.fold_in(own_key, 6)
    for dim, parts in split:
        steps = jnp.exp(jax.random.uniform(jax.random.fold_in(own, dim), (parts,), jnp.float32, low / len(split), top_value / len(split)))
        gain = gain * jnp.repeat(steps, extent[dim] // parts).reshape([-1 if axis == dim else 1 for axis in range(len(extent))])
    return gain


def scatter_about(stream_key, shape, scale, reach, split=(), kind=jnp.bfloat16):
    result = jax.random.normal(stream_key, shape, jnp.float32) * scale
    if len(split) > 0:
        result = steps_of(stream_key, shape, split, -0.22, 0.18) * result
    return jnp.clip(result, min=-reach, max=reach).astype(kind)


def setup_inputs(seed: int = 0) -> dict:
    key_list = jax.random.split(jax.random.key(seed), 4)
    queries = scatter_about(key_list[0], (SEQ, WIDTH), 1.0, 6.0, ((0, 32),))
    keys = scatter_about(key_list[1], (SEQ, WIDTH), 1.0, 6.0, ((0, 32),))
    values = scatter_about(key_list[2], (SEQ, WIDTH), 1.0, 6.0, ((0, 32),))
    return dict(queries=queries, keys=keys, values=values)


def reference(queries, keys, values):
    blocks = SEQ // TOK_DEV
    qs = queries.reshape(blocks, TOK_DEV, HEADS, HEAD_DIM)
    ks = keys.reshape(blocks, TOK_DEV, HEADS, HEAD_DIM)
    vs = values.reshape(blocks, TOK_DEV, HEADS, HEAD_DIM)
    rows = jnp.arange(TOK_DEV, dtype=jnp.int32)
    causal = rows[None, :, None] >= rows[None, None, :]

    def step(state, block):
        q_blk, k_blk, v_blk = block
        qf = q_blk.astype(jnp.float32)
        kf = k_blk.astype(jnp.float32)
        vf = v_blk.astype(jnp.float32)
        scores = jnp.einsum('thd,shd->hts', qf, kf)
        scores = jnp.where(causal, scores, 0.0).astype(jnp.bfloat16)
        local = jnp.einsum('hts,shd->thd', scores.astype(jnp.float32), vf)
        carried = jnp.einsum('thd,hde->the', qf, state, precision=lax.Precision.HIGHEST)
        total = local + carried
        scale = lax.rsqrt(lax.optimization_barrier(jnp.mean(total * total, axis=-1, keepdims=True)) + 1e-05)
        out = (total * scale).astype(jnp.bfloat16)
        new_state = state + jnp.einsum('shd,she->hde', kf, vf)
        return (new_state, out)
    start = jnp.zeros((HEADS, HEAD_DIM, HEAD_DIM), jnp.float32)
    _, outs = lax.scan(step, start, (qs, ks, vs))
    return outs.reshape(SEQ, HEADS * HEAD_DIM)
```

```python
import jax
import jax.numpy as jnp
from jax import lax
from jax.experimental import pallas as pl
from jax.experimental.pallas import tpu as pltpu
from jax.sharding import PartitionSpec as P

HEADS = 16
HEAD_DIM = 128
VMEM = pl.BlockSpec(memory_space=pltpu.VMEM)
LIMIT = 40 * 1024 * 1024


def call(kernel, outs, args, flops=0):
    moved = sum(a.size * a.dtype.itemsize for a in args)
    return pl.pallas_call(
        kernel,
        out_shape=outs,
        in_specs=[VMEM] * len(args),
        out_specs=jax.tree.map(lambda _: VMEM, outs),
        compiler_params=pltpu.CompilerParams(vmem_limit_bytes=LIMIT),
        cost_estimate=pl.CostEstimate(flops=flops, bytes_accessed=moved, transcendentals=0),
    )(*args)


def f32(*shape):
    return jax.ShapeDtypeStruct(shape, jnp.float32)


def half_states(keys, values, half, count):
    def kernel(k_ref, v_ref, s_ref):
        first = half() * (count * HEAD_DIM)
        for h in range(count):
            cols = pl.ds(pl.multiple_of(first + h * HEAD_DIM, HEAD_DIM), HEAD_DIM)
            s_ref[h] = lax.dot_general(
                k_ref[:, cols], v_ref[:, cols], (((0,), (0,)), ((), ())), preferred_element_type=jnp.float32
            )

    tokens = keys.shape[0]
    return call(
        kernel, f32(count, HEAD_DIM, HEAD_DIM), (keys, values), 2 * count * tokens * HEAD_DIM * HEAD_DIM
    )


def local_part(queries, keys, values):
    tokens = queries.shape[0]

    def kernel(q_ref, k_ref, v_ref, o_ref):
        rows = lax.broadcasted_iota(jnp.int32, (tokens, tokens), 0)
        cols = lax.broadcasted_iota(jnp.int32, (tokens, tokens), 1)
        causal = rows >= cols
        for h in range(HEADS):
            c = slice(h * HEAD_DIM, (h + 1) * HEAD_DIM)
            scores = lax.dot_general(
                q_ref[:, c], k_ref[:, c], (((1,), (1,)), ((), ())), preferred_element_type=jnp.float32
            )
            scores = jnp.where(causal, scores, 0.0).astype(jnp.bfloat16)
            o_ref[:, c] = jnp.dot(scores, v_ref[:, c], preferred_element_type=jnp.float32)

    return call(
        kernel, f32(tokens, HEADS * HEAD_DIM), (queries, keys, values), 4 * HEADS * tokens * tokens * HEAD_DIM
    )


def finish(queries, local, own, other, below_own, below_other):
    tokens = queries.shape[0]
    count = own.shape[0]

    def kernel(q_ref, l_ref, a_ref, b_ref, ba_ref, bb_ref, o_ref):
        mine = lax.axis_index("narrow")
        upper = mine.astype(jnp.float32)
        for part, (c_ref, below_ref) in enumerate(((a_ref, ba_ref), (b_ref, bb_ref))):
            first = (mine if part == 0 else 1 - mine) * (count * HEAD_DIM)
            for h in range(count):
                cols = pl.ds(pl.multiple_of(first + h * HEAD_DIM, HEAD_DIM), HEAD_DIM)
                carry = c_ref[h] + below_ref[h] * upper
                high = carry.astype(jnp.bfloat16)
                low = (carry - high.astype(jnp.float32)).astype(jnp.bfloat16)
                q = q_ref[:, cols]
                total = (
                    l_ref[:, cols]
                    + jnp.dot(q, high, preferred_element_type=jnp.float32)
                    + jnp.dot(q, low, preferred_element_type=jnp.float32)
                )
                factor = lax.rsqrt(jnp.mean(total * total, axis=-1, keepdims=True) + 1e-05)
                o_ref[:, cols] = (total * factor).astype(jnp.bfloat16)

    return call(
        kernel,
        jax.ShapeDtypeStruct(queries.shape, jnp.bfloat16),
        (queries, local, own, other, below_own, below_other),
        4 * HEADS * tokens * HEAD_DIM * HEAD_DIM,
    )


def prefixes(states, own, group):
    def kernel(x_ref, p_ref, t_ref):
        run = jnp.zeros(x_ref.shape[1:], jnp.float32)
        for i in range(group):
            p_ref[i] = run
            run = run + x_ref[i]
        t_ref[...] = run

    return call(kernel, (f32(*states.shape), f32(*states.shape[1:])), (states,))


def swap_cores(block):
    return lax.ppermute(block, "narrow", [(0, 1), (1, 0)])


def shards(queries, keys, values):
    chips = lax.axis_size("wide")
    count = HEADS // lax.axis_size("narrow")
    group = count
    groups = chips // group
    me = lax.axis_index("narrow")

    given = half_states(keys, values, lambda: 1 - lax.axis_index("narrow"), count)
    got = swap_cores(given)
    kept = half_states(keys, values, lambda: lax.axis_index("narrow"), count)
    below_other = swap_cores(kept)
    chip = kept + got
    cubes = [[g * group + r for r in range(group)] for g in range(groups)]
    theirs = lax.all_to_all(chip, "wide", 0, 0, axis_index_groups=cubes, tiled=True)
    before, running = prefixes(theirs, None, group)
    where = lax.axis_index("wide") // group
    earlier = jnp.zeros_like(running)
    step = 1
    while step < groups:
        route = [(i, i ^ (step * group)) for i in range(chips)]
        seen = lax.ppermute(running, "wide", route)
        earlier = earlier + jnp.where((where & step) != 0, seen, 0.0)
        running = running + seen
        step *= 2
    local = local_part(queries, keys, values)
    outer = lax.all_to_all(before + earlier, "wide", 0, 0, axis_index_groups=cubes, tiled=True)
    outer_other = swap_cores(outer)
    return finish(queries, local, outer, outer_other, got, below_other)


def solution(mesh):
    placed = P(("wide", "narrow"), None)
    return jax.shard_map(
        shards, mesh=mesh, in_specs=(placed, placed, placed), out_specs=placed, check_vma=False
    )
```

```python
import jax
import jax.numpy as jnp
from jax import lax
from jax.experimental import pallas as pl
from jax.experimental.pallas import tpu as pltpu
from jax.sharding import PartitionSpec as P

HEADS = 16
HEAD_DIM = 128
VMEM = pl.BlockSpec(memory_space=pltpu.VMEM)
HBM = pl.BlockSpec(memory_space=pltpu.HBM)
LIMIT = 8 * 1024 * 1024


def call(kernel, outs, args, flops=0, ins=None, out_specs=None, scratch=()):
    moved = sum(a.size * a.dtype.itemsize for a in args)
    return pl.pallas_call(
        kernel,
        out_shape=outs,
        in_specs=ins or [VMEM] * len(args),
        out_specs=out_specs or jax.tree.map(lambda _: VMEM, outs),
        scratch_shapes=scratch,
        compiler_params=pltpu.CompilerParams(vmem_limit_bytes=LIMIT),
        cost_estimate=pl.CostEstimate(flops=flops, bytes_accessed=moved, transcendentals=0),
    )(*args)


def f32(*shape):
    return jax.ShapeDtypeStruct(shape, jnp.float32)


def head(h, first=0):
    return pl.ds(pl.multiple_of(first + h * HEAD_DIM, HEAD_DIM), HEAD_DIM)


def half_states(keys, values, other, count, pieces=2):
    tokens = keys.shape[0]
    each = count // pieces
    width = each * HEAD_DIM

    def kernel(k_hbm, v_hbm, s_ref, k_ref, v_ref, sems):
        mine = lax.axis_index("narrow")
        first = (1 - mine if other else mine) * (count * HEAD_DIM)
        copies = []
        for p in range(pieces):
            cols = pl.ds(pl.multiple_of(first + p * width, width), width)
            for i, (src, dst) in enumerate(((k_hbm, k_ref), (v_hbm, v_ref))):
                copy = pltpu.make_async_copy(
                    src.at[:, cols], dst.at[:, p * width : (p + 1) * width], sems.at[p, i]
                )
                copy.start()
                copies.append(copy)
        for p in range(pieces):
            copies[2 * p].wait()
            copies[2 * p + 1].wait()
            for h in range(p * each, (p + 1) * each):
                cols = slice(h * HEAD_DIM, (h + 1) * HEAD_DIM)
                s_ref[h] = lax.dot_general(
                    k_ref[:, cols], v_ref[:, cols], (((0,), (0,)), ((), ())), preferred_element_type=jnp.float32
                )

    return call(
        kernel,
        f32(count, HEAD_DIM, HEAD_DIM),
        (pltpu.with_memory_space_constraint(keys, pltpu.HBM), pltpu.with_memory_space_constraint(values, pltpu.HBM)),
        2 * count * tokens * HEAD_DIM * HEAD_DIM,
        ins=[HBM, HBM],
        scratch=[
            pltpu.VMEM((tokens, count * HEAD_DIM), keys.dtype),
            pltpu.VMEM((tokens, count * HEAD_DIM), values.dtype),
            pltpu.SemaphoreType.DMA((pieces, 2)),
        ],
    )


def local_part(queries, keys, values):
    tokens = queries.shape[0]

    def kernel(q_ref, k_ref, v_ref, o_ref):
        rows = lax.broadcasted_iota(jnp.int32, (tokens, tokens), 0)
        cols = lax.broadcasted_iota(jnp.int32, (tokens, tokens), 1)
        causal = rows >= cols
        for h in range(HEADS):
            c = slice(h * HEAD_DIM, (h + 1) * HEAD_DIM)
            scores = lax.dot_general(
                q_ref[:, c], k_ref[:, c], (((1,), (1,)), ((), ())), preferred_element_type=jnp.float32
            )
            scores = jnp.where(causal, scores, 0.0).astype(jnp.bfloat16)
            o_ref[:, c] = jnp.dot(scores, v_ref[:, c], preferred_element_type=jnp.float32)

    return call(
        kernel, f32(tokens, HEADS * HEAD_DIM), (queries, keys, values), 4 * HEADS * tokens * tokens * HEAD_DIM
    )


def attended(q, local, carry):
    high = carry.astype(jnp.bfloat16)
    low = (carry - high.astype(jnp.float32)).astype(jnp.bfloat16)
    total = local + jnp.dot(
        jnp.concatenate([q, q], axis=1), jnp.concatenate([high, low], axis=0), preferred_element_type=jnp.float32
    )
    factor = lax.rsqrt(jnp.mean(total * total, axis=-1, keepdims=True) + 1e-05)
    return (total * factor).astype(jnp.bfloat16)


def finish_own(queries, local, outer, got):
    tokens = queries.shape[0]
    count = outer.shape[0]

    def kernel(q_ref, l_ref, c_ref, g_ref, o_ref):
        mine = lax.axis_index("narrow")
        for h in range(count):
            cols = head(h, mine * (count * HEAD_DIM))
            carry = c_ref[h] + jnp.where(mine == 1, g_ref[h], 0.0)
            o_ref[:, h * HEAD_DIM : (h + 1) * HEAD_DIM] = attended(q_ref[:, cols], l_ref[:, cols], carry)

    return call(
        kernel,
        jax.ShapeDtypeStruct((tokens, count * HEAD_DIM), jnp.bfloat16),
        (queries, local, outer, got),
        4 * count * tokens * HEAD_DIM * HEAD_DIM,
    )


def finish_other(queries, local, carry, done, pieces=2):
    tokens = queries.shape[0]
    count = carry.shape[0]
    each = count // pieces
    width = each * HEAD_DIM

    def kernel(q_ref, l_ref, c_ref, d_ref, o_hbm, y_ref, sems):
        mine = lax.axis_index("narrow")
        half = count * HEAD_DIM
        copies = [
            pltpu.make_async_copy(d_ref, o_hbm.at[:, pl.ds(pl.multiple_of(mine * half, half), half)], sems.at[pieces])
        ]
        copies[0].start()
        first = (1 - mine) * half
        for p in range(pieces):
            for h in range(p * each, (p + 1) * each):
                cols = head(h, first)
                y_ref[:, h * HEAD_DIM : (h + 1) * HEAD_DIM] = attended(q_ref[:, cols], l_ref[:, cols], c_ref[h])
            copy = pltpu.make_async_copy(
                y_ref.at[:, p * width : (p + 1) * width],
                o_hbm.at[:, pl.ds(pl.multiple_of(first + p * width, width), width)],
                sems.at[p],
            )
            copy.start()
            copies.append(copy)
        for copy in copies:
            copy.wait()

    return call(
        kernel,
        jax.ShapeDtypeStruct(queries.shape, jnp.bfloat16),
        (queries, local, carry, done),
        4 * count * tokens * HEAD_DIM * HEAD_DIM,
        out_specs=HBM,
        scratch=[
            pltpu.VMEM((tokens, count * HEAD_DIM), jnp.bfloat16),
            pltpu.SemaphoreType.DMA((pieces + 1,)),
        ],
    )


def sum_of(states):
    def kernel(x_ref, t_ref):
        run = x_ref[0]
        for i in range(1, states.shape[0]):
            run = run + x_ref[i]
        t_ref[...] = run

    return call(kernel, f32(*states.shape[1:]), (states,))


def prefixes(states, start):
    def kernel(x_ref, s_ref, p_ref):
        run = s_ref[...]
        for i in range(states.shape[0]):
            p_ref[i] = run
            if i + 1 < states.shape[0]:
                run = run + x_ref[i]

    return call(kernel, f32(*states.shape), (states, start))


def add_lower(outer, kept):
    def kernel(a_ref, b_ref, o_ref):
        lower = lax.axis_index("narrow") == 0
        for h in range(outer.shape[0]):
            o_ref[h] = a_ref[h] + jnp.where(lower, b_ref[h], 0.0)

    return call(kernel, f32(*outer.shape), (outer, kept))


def swap_cores(block):
    return lax.ppermute(block, "narrow", [(0, 1), (1, 0)])


def shards(queries, keys, values):
    chips = lax.axis_size("wide")
    count = HEADS // lax.axis_size("narrow")
    group = count
    groups = chips // group
    cubes = [[g * group + r for r in range(group)] for g in range(groups)]

    given = half_states(keys, values, True, count)
    got = swap_cores(given)
    kept = half_states(keys, values, False, count)
    chip = kept + got
    theirs = lax.all_to_all(chip, "wide", 0, 0, axis_index_groups=cubes, tiled=True)

    cube = lax.axis_index("wide") // group
    running = sum_of(theirs)
    later_q, _ = lax.optimization_barrier((queries, running))
    local = local_part(later_q, keys, values)
    earlier = None
    step = 1
    while step < groups:
        seen = lax.ppermute(running, "wide", [(i, i ^ (step * group)) for i in range(chips)])
        lower = jnp.where((cube & step) != 0, seen, 0.0)
        earlier = lower if earlier is None else earlier + lower
        running = running + seen
        step *= 2
    earlier, local = lax.optimization_barrier((earlier, local))
    outer = lax.all_to_all(prefixes(theirs, earlier), "wide", 0, 0, axis_index_groups=cubes, tiled=True)
    other = swap_cores(add_lower(outer, kept))
    own = finish_own(queries, local, outer, got)
    return finish_other(queries, local, other, own)


def solution(mesh):
    placed = P(("wide", "narrow"), None)
    return jax.shard_map(
        shards, mesh=mesh, in_specs=(placed, placed, placed), out_specs=placed, check_vma=False
    )
```

```python
import jax
import jax.numpy as jnp
from jax import lax
from jax.experimental import pallas as pl
from jax.experimental.pallas import tpu as pltpu
from jax.sharding import PartitionSpec as P

HEADS = 16
HEAD_DIM = 128
VMEM = pl.BlockSpec(memory_space=pltpu.VMEM)
HBM = pl.BlockSpec(memory_space=pltpu.HBM)
NEAR = 1
TURNS = (6, 4, 2)
LIMIT = 8 * 1024 * 1024


def call(kernel, outs, args, flops=0, ins=None, out_specs=None, scratch=()):
    moved = sum(a.size * a.dtype.itemsize for a in args)
    return pl.pallas_call(
        kernel,
        out_shape=outs,
        in_specs=ins or [VMEM] * len(args),
        out_specs=out_specs or ([VMEM] * len(outs) if isinstance(outs, list) else VMEM),
        scratch_shapes=scratch,
        compiler_params=pltpu.CompilerParams(vmem_limit_bytes=LIMIT),
        cost_estimate=pl.CostEstimate(flops=flops, bytes_accessed=moved, transcendentals=0),
    )(*args)


def f32(*shape):
    return pltpu.VMEM(shape, jnp.float32)


def head(h, first=0):
    return pl.ds(pl.multiple_of(first + h * HEAD_DIM, HEAD_DIM), HEAD_DIM)


def place_in_cube(group):
    return lax.rem(lax.axis_index("wide"), group)


def partner(core, turn, group):
    return TURNS[turn] ^ (NEAR * core)


def turns_of(group):
    return (group - 2) // 2


def heads_of(core, place, group):
    heads = []
    for turn in range(turns_of(group)):
        owner = place ^ partner(core, turn, group)
        heads += [owner, group + owner]
    return heads + [core * group + (place ^ NEAR), core * group + place]


def first_states(keys, values, group):
    tokens, width = keys.shape
    part = width // 2

    def kernel(k_hbm, v_hbm, s_ref, k_ref, v_ref, sems):
        copies = []
        for n in range(2):
            cols = slice(n * part, (n + 1) * part)
            for i, (src, dst) in enumerate(((k_hbm, k_ref), (v_hbm, v_ref))):
                copies.append(pltpu.make_async_copy(src.at[:, cols], dst.at[:, cols], sems.at[n, i]))
                copies[-1].start()
        for copy in copies:
            copy.wait()
        for n, h in enumerate(heads_of(1 - lax.axis_index("narrow"), place_in_cube(group), group)):
            s_ref[n] = state(k_ref[:, head(h)], v_ref[:, head(h)])

    return call(
        kernel,
        [f32(group, HEAD_DIM, HEAD_DIM)] + [pltpu.VMEM(keys.shape, keys.dtype)] * 2,
        (pltpu.with_memory_space_constraint(keys, pltpu.HBM), pltpu.with_memory_space_constraint(values, pltpu.HBM)),
        2 * group * tokens * HEAD_DIM * HEAD_DIM,
        ins=[HBM, HBM],
        scratch=[pltpu.SemaphoreType.DMA((2, 2))],
    )


def kept_states(keys, values, group):
    tokens = keys.shape[0]

    def kernel(k_ref, v_ref, s_ref):
        for n, h in enumerate(heads_of(lax.axis_index("narrow"), place_in_cube(group), group)):
            s_ref[n] = state(k_ref[:, head(h)], v_ref[:, head(h)])

    return call(
        kernel, f32(group, HEAD_DIM, HEAD_DIM), (keys, values), 2 * group * tokens * HEAD_DIM * HEAD_DIM
    )


def state(k, v):
    return lax.dot_general(k, v, (((0,), (0,)), ((), ())), preferred_element_type=jnp.float32)


def local_part(queries, keys, values):
    tokens = queries.shape[0]

    def kernel(q_ref, k_ref, v_ref, o_ref):
        rows = lax.broadcasted_iota(jnp.int32, (tokens, tokens), 0)
        cols = lax.broadcasted_iota(jnp.int32, (tokens, tokens), 1)
        causal = rows >= cols
        for h in range(HEADS):
            c = slice(h * HEAD_DIM, (h + 1) * HEAD_DIM)
            scores = lax.dot_general(
                q_ref[:, c], k_ref[:, c], (((1,), (1,)), ((), ())), preferred_element_type=jnp.float32
            )
            scores = jnp.where(causal, scores, 0.0).astype(jnp.bfloat16)
            o_ref[:, c] = jnp.dot(scores, v_ref[:, c], preferred_element_type=jnp.float32)

    return call(
        kernel, f32(tokens, HEADS * HEAD_DIM), (queries, keys, values), 4 * HEADS * tokens * tokens * HEAD_DIM
    )


def attended(q, local, carry):
    high = carry.astype(jnp.bfloat16)
    low = (carry - high.astype(jnp.float32)).astype(jnp.bfloat16)
    total = local + jnp.dot(
        jnp.concatenate([q, q], axis=1), jnp.concatenate([high, low], axis=0), preferred_element_type=jnp.float32
    )
    factor = lax.rsqrt(jnp.mean(total * total, axis=-1, keepdims=True) + 1e-05)
    return (total * factor).astype(jnp.bfloat16)


def finish_own(queries, local, pieces, got, group):
    tokens = queries.shape[0]
    turns = turns_of(group)

    def kernel(q_ref, l_ref, g_ref, *refs):
        o_ref = refs[-1]
        core = lax.axis_index("narrow")
        for n, h in enumerate(heads_of(core, place_in_cube(group), group)):
            carry = piece(refs, n, turns) + jnp.where(core == 1, g_ref[n], 0.0)
            o_ref[:, n * HEAD_DIM : (n + 1) * HEAD_DIM] = attended(q_ref[:, head(h)], l_ref[:, head(h)], carry)

    return call(
        kernel,
        pltpu.VMEM((tokens, group * HEAD_DIM), jnp.bfloat16),
        (queries, local, got, *pieces),
        4 * group * tokens * HEAD_DIM * HEAD_DIM,
    )


def finish_other(queries, local, carry, done, group, parts=2):
    tokens = queries.shape[0]
    rows = tokens // parts

    def kernel(q_ref, l_ref, c_ref, d_ref, o_hbm, y_ref, sems):
        core, place = lax.axis_index("narrow"), place_in_cube(group)
        for n, h in enumerate(heads_of(core, place, group)):
            y_ref[:, head(h)] = d_ref[:, n * HEAD_DIM : (n + 1) * HEAD_DIM]
        copies = []
        for p in range(parts):
            some = slice(p * rows, (p + 1) * rows)
            for n, h in enumerate(heads_of(1 - core, place, group)):
                y_ref[some, head(h)] = attended(q_ref[some, head(h)], l_ref[some, head(h)], c_ref[n])
            copies.append(pltpu.make_async_copy(y_ref.at[some, :], o_hbm.at[some, :], sems.at[p]))
            copies[-1].start()
        for copy in copies:
            copy.wait()

    return call(
        kernel,
        jax.ShapeDtypeStruct(queries.shape, jnp.bfloat16),
        (queries, local, carry, done),
        4 * group * tokens * HEAD_DIM * HEAD_DIM,
        out_specs=HBM,
        scratch=[pltpu.VMEM(queries.shape, jnp.bfloat16), pltpu.SemaphoreType.DMA((parts,))],
    )


def piece(refs, n, turns):
    return refs[n // 2][n % 2] if n < 2 * turns else refs[n - turns][...]


def chip_pieces(kept, got):
    group = kept.shape[0]
    turns = turns_of(group)

    def kernel(a_ref, b_ref, *o_refs):
        for turn in range(turns):
            for n in range(2):
                o_refs[turn][n] = a_ref[2 * turn + n] + b_ref[2 * turn + n]
        o_refs[turns][...] = a_ref[group - 2] + b_ref[group - 2]
        o_refs[turns + 1][...] = a_ref[group - 1] + b_ref[group - 1]

    shape = kept.shape[1:]
    return call(kernel, [f32(2, *shape)] * turns + [f32(*shape)] * 2, (kept, got))


def for_other_core(pairs):
    def kernel(*refs):
        other = 1 - lax.axis_index("narrow")
        for n, ref in enumerate(refs[:-1]):
            refs[-1][n] = ref[other]

    return call(kernel, f32(len(pairs), *pairs[0].shape[1:]), pairs)


def ends(core, own, far):
    return jnp.where(core == 0, own, far), jnp.where(core == 0, far, own)


def gathered(pairs, swapped, near, own):
    turns = len(pairs)

    def kernel(*refs):
        pair_refs, (s_ref, far_ref, own_ref, t_ref, p_ref) = refs[:turns], refs[turns:]
        core = lax.axis_index("narrow")
        own, far = own_ref[...], far_ref[...]
        p_ref[turns], p_ref[turns + 1] = ends(core, own, far)
        run = own + far
        for turn in range(turns):
            mine = pair_refs[turn][core]
            p_ref[turn] = mine
            run = run + mine + s_ref[turn]
        t_ref[...] = run

    shape = own.shape
    return call(kernel, [f32(*shape), f32(turns + 2, *shape)], (*pairs, swapped, near, own))


def prefix_at(blocks, corner, k):
    total, sums, bit = 0.0, blocks, 0
    while len(sums) > 1:
        inside = ((corner ^ k) >> bit & 1).astype(jnp.float32)
        total = total + sums[(k >> bit) ^ 1] * inside
        sums = [sums[i] + sums[i + 1] for i in range(0, len(sums), 2)]
        bit += 1
    return total


def cube_prefixes(pairs, swapped, near, own, received, group):
    turns = turns_of(group)
    rows = own.shape[0] // 4

    def kernel(*refs):
        pair_refs, (s_ref, far_ref, own_ref, r_ref) = refs[:turns], refs[turns : turns + 4]
        outs = refs[turns + 4 :]
        core, place = lax.axis_index("narrow"), place_in_cube(group)
        corner = place ^ (NEAR * core)
        for part in range(4):
            some = slice(part * rows, (part + 1) * rows)
            mine, other = [None] * group, [None] * group
            mine[0], mine[NEAR] = ends(core, own_ref[some], far_ref[some])
            other[NEAR], other[0] = r_ref[turns, some], r_ref[turns + 1, some]
            for turn in range(turns):
                mine[TURNS[turn]] = pair_refs[turn][core, some]
                mine[NEAR ^ TURNS[turn]] = s_ref[turn, some]
                other[TURNS[turn]] = pair_refs[turn][1 - core, some]
                other[NEAR ^ TURNS[turn]] = r_ref[turn, some]
            for turn in range(turns):
                outs[turn][core, some] = prefix_at(mine, corner, TURNS[turn])
                outs[turn][1 - core, some] = prefix_at(other, corner, TURNS[turn])
            own_sum, far_sum = ends(core, prefix_at(mine, corner, 0), prefix_at(mine, corner, NEAR))
            outs[turns][some] = far_sum
            outs[turns + 1][some] = own_sum

    shape = own.shape
    return call(
        kernel, [f32(2, *shape)] * turns + [f32(*shape)] * 2, (*pairs, swapped, near, own, received)
    )


def add_earlier(pieces, earlier, others, upper_only, group):
    count = len(pieces)

    def kernel(e_ref, o_ref, *refs):
        core = lax.axis_index("narrow")
        mine, other = e_ref[...], o_ref[...]
        if upper_only:
            upper = lax.axis_index("wide") >= group
            mine, other = jnp.where(upper, mine, 0.0), jnp.where(upper, other, 0.0)
        for ref, out in zip(refs[:count], refs[count:]):
            if len(ref.shape) == 3:
                out[core] = ref[core] + mine
                out[1 - core] = ref[1 - core] + other
            else:
                out[...] = ref[...] + mine

    return call(kernel, [f32(*piece.shape) for piece in pieces], (earlier, others, *pieces))


def add_lower(pieces, kept):
    group = kept.shape[0]
    turns = turns_of(group)

    def kernel(k_ref, *refs):
        lower = lax.axis_index("narrow") == 0
        for n in range(group):
            refs[-1][n] = piece(refs, n, turns) + jnp.where(lower, k_ref[n], 0.0)

    return call(kernel, f32(*kept.shape), (kept, *pieces))


def swap_cores(block):
    return lax.ppermute(block, "narrow", [(0, 1), (1, 0)])


def pair_chips(block, chips, cores, of):
    route = [(i * cores + c, (i ^ of(c)) * cores + c) for i in range(chips) for c in range(cores)]
    return lax.ppermute(block, ("wide", "narrow"), route)


def pairings(pairs, near, chips, cores, group):
    pairs = [
        pair_chips(pair, chips, cores, lambda c, turn=turn: partner(c, turn, group)) for turn, pair in enumerate(pairs)
    ]
    return pairs, pair_chips(near, chips, cores, lambda c: NEAR)


def shards(queries, keys, values):
    chips, cores = lax.axis_size("wide"), lax.axis_size("narrow")
    group = HEADS // cores
    groups = chips // group

    given, keys, values = first_states(keys, values, group)
    got = swap_cores(given)
    kept = kept_states(keys, values, group)
    *pairs, near, mine = chip_pieces(kept, got)
    later_q, _ = lax.optimization_barrier((queries, mine))
    pairs, near = pairings(pairs, near, chips, cores, group)
    local = local_part(later_q, keys, values)
    *pairs, near, local = lax.optimization_barrier((*pairs, near, local))
    swapped = swap_cores(for_other_core(pairs))
    running, lacking = gathered(pairs, swapped, near, mine)
    cube = lax.axis_index("wide") // group
    earlier = jnp.zeros_like(running) if groups != 2 else None
    step = 1
    while step < groups:
        seen = lax.ppermute(running, "wide", [(i, i ^ (step * group)) for i in range(chips)])
        earlier = seen if groups == 2 else earlier + jnp.where((cube & step) != 0, seen, 0.0)
        running = running + seen
        step *= 2
    received = swap_cores(lacking)
    earlier, received = lax.optimization_barrier((earlier, received))
    others = swap_cores(earlier)
    pieces = cube_prefixes(pairs, swapped, near, mine, received, group)
    others, *pieces = lax.optimization_barrier((others, *pieces))
    *pairs, far, mine = add_earlier(pieces, earlier, others, groups == 2, group)
    pairs, far = pairings(pairs, far, chips, cores, group)
    pieces = lax.optimization_barrier((*pairs, far, mine))
    other = swap_cores(add_lower(pieces, kept))
    own = finish_own(queries, local, pieces, got, group)
    return finish_other(queries, local, other, own, group)


def solution(mesh):
    placed = P(("wide", "narrow"), None)
    return jax.shard_map(
        shards, mesh=mesh, in_specs=(placed, placed, placed), out_specs=placed, check_vma=False
    )
```

```python
import jax
import jax.numpy as jnp
from jax import lax
from jax.experimental import pallas as pl
from jax.experimental.pallas import tpu as pltpu
from jax.sharding import PartitionSpec as P

HEADS = 16
HEAD_DIM = 128
VMEM = pl.BlockSpec(memory_space=pltpu.VMEM)
HBM = pl.BlockSpec(memory_space=pltpu.HBM)
NEAR = 1
LIMIT = 8 * 1024 * 1024


def call(kernel, outs, args, flops=0, ins=None, out_specs=None, scratch=()):
    moved = sum(a.size * a.dtype.itemsize for a in args)
    return pl.pallas_call(
        kernel,
        out_shape=outs,
        in_specs=ins or [VMEM] * len(args),
        out_specs=out_specs or ([VMEM] * len(outs) if isinstance(outs, list) else VMEM),
        scratch_shapes=scratch,
        compiler_params=pltpu.CompilerParams(vmem_limit_bytes=LIMIT),
        cost_estimate=pl.CostEstimate(flops=flops, bytes_accessed=moved, transcendentals=0),
    )(*args)


def f32(*shape):
    return pltpu.VMEM(shape, jnp.float32)


def head(h, first=0):
    return pl.ds(pl.multiple_of(first + h * HEAD_DIM, HEAD_DIM), HEAD_DIM)


def place_in_cube(group):
    return lax.rem(lax.axis_index("wide"), group)


def partner(core, turn, group):
    return (group - 2 * (turn + 1)) ^ (NEAR * core)


def turns_of(group):
    return (group - 2) // 2


def heads_of(core, place, group):
    heads = []
    for turn in range(turns_of(group)):
        owner = place ^ partner(core, turn, group)
        heads += [owner, group + owner]
    return heads + [core * group + (place ^ NEAR), core * group + place]


def first_states(keys, values, group):
    tokens, width = keys.shape
    part = width // 2

    def kernel(k_hbm, v_hbm, s_ref, k_ref, v_ref, sems):
        copies = []
        for n in range(2):
            cols = slice(n * part, (n + 1) * part)
            for i, (src, dst) in enumerate(((k_hbm, k_ref), (v_hbm, v_ref))):
                copies.append(pltpu.make_async_copy(src.at[:, cols], dst.at[:, cols], sems.at[n, i]))
                copies[-1].start()
        for copy in copies:
            copy.wait()
        for n, h in enumerate(heads_of(1 - lax.axis_index("narrow"), place_in_cube(group), group)):
            s_ref[n] = state(k_ref[:, head(h)], v_ref[:, head(h)])

    return call(
        kernel,
        [f32(group, HEAD_DIM, HEAD_DIM)] + [pltpu.VMEM(keys.shape, keys.dtype)] * 2,
        (pltpu.with_memory_space_constraint(keys, pltpu.HBM), pltpu.with_memory_space_constraint(values, pltpu.HBM)),
        2 * group * tokens * HEAD_DIM * HEAD_DIM,
        ins=[HBM, HBM],
        scratch=[pltpu.SemaphoreType.DMA((2, 2))],
    )


def kept_states(keys, values, group):
    tokens = keys.shape[0]

    def kernel(k_ref, v_ref, s_ref):
        for n, h in enumerate(heads_of(lax.axis_index("narrow"), place_in_cube(group), group)):
            s_ref[n] = state(k_ref[:, head(h)], v_ref[:, head(h)])

    return call(
        kernel, f32(group, HEAD_DIM, HEAD_DIM), (keys, values), 2 * group * tokens * HEAD_DIM * HEAD_DIM
    )


def state(k, v):
    return lax.dot_general(k, v, (((0,), (0,)), ((), ())), preferred_element_type=jnp.float32)


def local_part(queries, keys, values):
    tokens = queries.shape[0]

    def kernel(q_ref, k_ref, v_ref, o_ref):
        rows = lax.broadcasted_iota(jnp.int32, (tokens, tokens), 0)
        cols = lax.broadcasted_iota(jnp.int32, (tokens, tokens), 1)
        causal = rows >= cols
        for h in range(HEADS):
            c = slice(h * HEAD_DIM, (h + 1) * HEAD_DIM)
            scores = lax.dot_general(
                q_ref[:, c], k_ref[:, c], (((1,), (1,)), ((), ())), preferred_element_type=jnp.float32
            )
            scores = jnp.where(causal, scores, 0.0).astype(jnp.bfloat16)
            o_ref[:, c] = jnp.dot(scores, v_ref[:, c], preferred_element_type=jnp.float32)

    return call(
        kernel, f32(tokens, HEADS * HEAD_DIM), (queries, keys, values), 4 * HEADS * tokens * tokens * HEAD_DIM
    )


def attended(q, local, carry):
    high = carry.astype(jnp.bfloat16)
    low = (carry - high.astype(jnp.float32)).astype(jnp.bfloat16)
    total = local + jnp.dot(
        jnp.concatenate([q, q], axis=1), jnp.concatenate([high, low], axis=0), preferred_element_type=jnp.float32
    )
    factor = lax.rsqrt(jnp.mean(total * total, axis=-1, keepdims=True) + 1e-05)
    return (total * factor).astype(jnp.bfloat16)


def finish_own(queries, local, pieces, got, group):
    tokens = queries.shape[0]
    turns = turns_of(group)

    def kernel(q_ref, l_ref, g_ref, *refs):
        o_ref = refs[-1]
        core = lax.axis_index("narrow")
        for n, h in enumerate(heads_of(core, place_in_cube(group), group)):
            carry = piece(refs, n, turns) + jnp.where(core == 1, g_ref[n], 0.0)
            o_ref[:, n * HEAD_DIM : (n + 1) * HEAD_DIM] = attended(q_ref[:, head(h)], l_ref[:, head(h)], carry)

    return call(
        kernel,
        pltpu.VMEM((tokens, group * HEAD_DIM), jnp.bfloat16),
        (queries, local, got, *pieces),
        4 * group * tokens * HEAD_DIM * HEAD_DIM,
    )


def finish_other(queries, local, carry, done, group, parts=2):
    tokens = queries.shape[0]
    rows = tokens // parts

    def kernel(q_ref, l_ref, c_ref, d_ref, o_hbm, y_ref, sems):
        core, place = lax.axis_index("narrow"), place_in_cube(group)
        for n, h in enumerate(heads_of(core, place, group)):
            y_ref[:, head(h)] = d_ref[:, n * HEAD_DIM : (n + 1) * HEAD_DIM]
        copies = []
        for p in range(parts):
            some = slice(p * rows, (p + 1) * rows)
            for n, h in enumerate(heads_of(1 - core, place, group)):
                y_ref[some, head(h)] = attended(q_ref[some, head(h)], l_ref[some, head(h)], c_ref[n])
            copies.append(pltpu.make_async_copy(y_ref.at[some, :], o_hbm.at[some, :], sems.at[p]))
            copies[-1].start()
        for copy in copies:
            copy.wait()

    return call(
        kernel,
        jax.ShapeDtypeStruct(queries.shape, jnp.bfloat16),
        (queries, local, carry, done),
        4 * group * tokens * HEAD_DIM * HEAD_DIM,
        out_specs=HBM,
        scratch=[pltpu.VMEM(queries.shape, jnp.bfloat16), pltpu.SemaphoreType.DMA((parts,))],
    )


def piece(refs, n, turns):
    return refs[n // 2][n % 2] if n < 2 * turns else refs[n - turns][...]


def chip_pieces(kept, got):
    group = kept.shape[0]
    turns = turns_of(group)

    def kernel(a_ref, b_ref, *o_refs):
        for turn in range(turns):
            for n in range(2):
                o_refs[turn][n] = a_ref[2 * turn + n] + b_ref[2 * turn + n]
        o_refs[turns][...] = a_ref[group - 2] + b_ref[group - 2]
        o_refs[turns + 1][...] = a_ref[group - 1] + b_ref[group - 1]

    shape = kept.shape[1:]
    return call(kernel, [f32(2, *shape)] * turns + [f32(*shape)] * 2, (kept, got))


def for_other_core(pairs):
    def kernel(*refs):
        other = 1 - lax.axis_index("narrow")
        for n, ref in enumerate(refs[:-1]):
            refs[-1][n] = ref[other]

    return call(kernel, f32(len(pairs), *pairs[0].shape[1:]), pairs)


def ends(core, own, far):
    return jnp.where(core == 0, own, far), jnp.where(core == 0, far, own)


def gathered(pairs, swapped, near, own):
    turns = len(pairs)

    def kernel(*refs):
        pair_refs, (s_ref, far_ref, own_ref, t_ref, p_ref) = refs[:turns], refs[turns:]
        core = lax.axis_index("narrow")
        own, far = own_ref[...], far_ref[...]
        p_ref[turns], p_ref[turns + 1] = ends(core, own, far)
        run = own + far
        for turn in range(turns):
            mine = pair_refs[turn][core]
            p_ref[turn] = mine
            run = run + mine + s_ref[turn]
        t_ref[...] = run

    shape = own.shape
    return call(kernel, [f32(*shape), f32(turns + 2, *shape)], (*pairs, swapped, near, own))


def prefix_at(blocks, corner, k):
    total, sums, bit = 0.0, blocks, 0
    while len(sums) > 1:
        inside = ((corner ^ k) >> bit & 1).astype(jnp.float32)
        total = total + sums[(k >> bit) ^ 1] * inside
        sums = [sums[i] + sums[i + 1] for i in range(0, len(sums), 2)]
        bit += 1
    return total


def cube_prefixes(pairs, swapped, near, own, received, group):
    turns = turns_of(group)
    rows = own.shape[0] // 4

    def kernel(*refs):
        pair_refs, (s_ref, far_ref, own_ref, r_ref) = refs[:turns], refs[turns : turns + 4]
        outs = refs[turns + 4 :]
        core, place = lax.axis_index("narrow"), place_in_cube(group)
        corner = place ^ (NEAR * core)
        for part in range(4):
            some = slice(part * rows, (part + 1) * rows)
            mine, other = [None] * group, [None] * group
            mine[0], mine[NEAR] = ends(core, own_ref[some], far_ref[some])
            other[NEAR], other[0] = r_ref[turns, some], r_ref[turns + 1, some]
            for turn in range(turns):
                mine[partner(0, turn, group)] = pair_refs[turn][core, some]
                mine[NEAR ^ partner(0, turn, group)] = s_ref[turn, some]
                other[partner(0, turn, group)] = pair_refs[turn][1 - core, some]
                other[NEAR ^ partner(0, turn, group)] = r_ref[turn, some]
            for turn in range(turns):
                outs[turn][core, some] = prefix_at(mine, corner, partner(0, turn, group))
                outs[turn][1 - core, some] = prefix_at(other, corner, partner(0, turn, group))
            own_sum, far_sum = ends(core, prefix_at(mine, corner, 0), prefix_at(mine, corner, NEAR))
            outs[turns][some] = far_sum
            outs[turns + 1][some] = own_sum

    shape = own.shape
    return call(
        kernel, [f32(2, *shape)] * turns + [f32(*shape)] * 2, (*pairs, swapped, near, own, received)
    )


def add_earlier(pieces, earlier, others, upper_only, group):
    count = len(pieces)

    def kernel(e_ref, o_ref, *refs):
        core = lax.axis_index("narrow")
        mine, other = e_ref[...], o_ref[...]
        if upper_only:
            upper = lax.axis_index("wide") >= group
            mine, other = jnp.where(upper, mine, 0.0), jnp.where(upper, other, 0.0)
        for ref, out in zip(refs[:count], refs[count:]):
            if len(ref.shape) == 3:
                out[core] = ref[core] + mine
                out[1 - core] = ref[1 - core] + other
            else:
                out[...] = ref[...] + mine

    return call(kernel, [f32(*piece.shape) for piece in pieces], (earlier, others, *pieces))


def add_lower(pieces, kept):
    group = kept.shape[0]
    turns = turns_of(group)

    def kernel(k_ref, *refs):
        lower = lax.axis_index("narrow") == 0
        for n in range(group):
            refs[-1][n] = piece(refs, n, turns) + jnp.where(lower, k_ref[n], 0.0)

    return call(kernel, f32(*kept.shape), (kept, *pieces))


def swap_cores(block):
    return lax.ppermute(block, "narrow", [(0, 1), (1, 0)])


def pair_chips(block, chips, cores, of):
    route = [(i * cores + c, (i ^ of(c)) * cores + c) for i in range(chips) for c in range(cores)]
    return lax.ppermute(block, ("wide", "narrow"), route)


def pairings(pairs, near, chips, cores, group):
    pairs = [
        pair_chips(pair, chips, cores, lambda c, turn=turn: partner(c, turn, group)) for turn, pair in enumerate(pairs)
    ]
    return pairs, pair_chips(near, chips, cores, lambda c: NEAR)


def shards(queries, keys, values):
    chips, cores = lax.axis_size("wide"), lax.axis_size("narrow")
    group = HEADS // cores
    groups = chips // group

    given, keys, values = first_states(keys, values, group)
    got = swap_cores(given)
    kept = kept_states(keys, values, group)
    *pairs, near, mine = chip_pieces(kept, got)
    later_q, _ = lax.optimization_barrier((queries, mine))
    pairs, near = pairings(pairs, near, chips, cores, group)
    local = local_part(later_q, keys, values)
    *pairs, near, local = lax.optimization_barrier((*pairs, near, local))
    swapped = swap_cores(for_other_core(pairs))
    running, lacking = gathered(pairs, swapped, near, mine)
    cube = lax.axis_index("wide") // group
    earlier = jnp.zeros_like(running) if groups != 2 else None
    step = 1
    while step < groups:
        seen = lax.ppermute(running, "wide", [(i, i ^ (step * group)) for i in range(chips)])
        earlier = seen if groups == 2 else earlier + jnp.where((cube & step) != 0, seen, 0.0)
        running = running + seen
        step *= 2
    received = swap_cores(lacking)
    earlier, received = lax.optimization_barrier((earlier, received))
    others = swap_cores(earlier)
    pieces = cube_prefixes(pairs, swapped, near, mine, received, group)
    others, *pieces = lax.optimization_barrier((others, *pieces))
    *pairs, far, mine = add_earlier(pieces, earlier, others, groups == 2, group)
    pairs, far = pairings(pairs, far, chips, cores, group)
    pieces = lax.optimization_barrier((*pairs, far, mine))
    other = swap_cores(add_lower(pieces, kept))
    own = finish_own(queries, local, pieces, got, group)
    return finish_other(queries, local, other, own, group)


def solution(mesh):
    placed = P(("wide", "narrow"), None)
    return jax.shard_map(
        shards, mesh=mesh, in_specs=(placed, placed, placed), out_specs=placed, check_vma=False
    )
```

```python
import jax
import jax.numpy as jnp
from jax import lax
from jax.experimental import pallas as pl
from jax.experimental.pallas import tpu as pltpu
from jax.sharding import PartitionSpec as P

HEADS = 16
HEAD_DIM = 128
VMEM = pl.BlockSpec(memory_space=pltpu.VMEM)
HBM = pl.BlockSpec(memory_space=pltpu.HBM)
NEAR = 1
LIMIT = 8 * 1024 * 1024


def call(kernel, outs, args, flops=0, ins=None, out_specs=None, scratch=(), aliases={}):
    moved = sum(a.size * a.dtype.itemsize for a in args)
    return pl.pallas_call(
        kernel,
        out_shape=outs,
        in_specs=ins or [VMEM] * len(args),
        out_specs=out_specs or ([VMEM] * len(outs) if isinstance(outs, list) else VMEM),
        scratch_shapes=scratch,
        input_output_aliases=aliases,
        compiler_params=pltpu.CompilerParams(vmem_limit_bytes=LIMIT),
        cost_estimate=pl.CostEstimate(flops=flops, bytes_accessed=moved, transcendentals=0),
    )(*args)


def f32(*shape):
    return pltpu.VMEM(shape, jnp.float32)


def head(h, first=0):
    return pl.ds(pl.multiple_of(first + h * HEAD_DIM, HEAD_DIM), HEAD_DIM)


def place_in_cube(group):
    return lax.rem(lax.axis_index("wide"), group)


def partner(core, turn, group):
    return (group - 2 * (turn + 1)) ^ (NEAR * core)


def turns_of(group):
    return (group - 2) // 2


def heads_of(core, place, group):
    heads = []
    for turn in range(turns_of(group)):
        owner = place ^ partner(core, turn, group)
        heads += [owner, group + owner]
    return heads + [core * group + (place ^ NEAR), core * group + place]


def first_states(keys, values, group):
    tokens, width = keys.shape
    part = width // 2

    def kernel(k_hbm, v_hbm, s_ref, k_ref, v_ref, sems):
        copies = []
        for n in range(2):
            cols = slice(n * part, (n + 1) * part)
            for i, (src, dst) in enumerate(((k_hbm, k_ref), (v_hbm, v_ref))):
                copies.append(pltpu.make_async_copy(src.at[:, cols], dst.at[:, cols], sems.at[n, i]))
                copies[-1].start()
        heads = heads_of(1 - lax.axis_index("narrow"), place_in_cube(group), group)
        lower = [2 * turn for turn in range(turns_of(group))]
        for n in range(2):
            copies[2 * n].wait()
            copies[2 * n + 1].wait()
            for m in lower if n == 0 else [m for m in range(group) if m not in lower]:
                s_ref[m] = state(k_ref[:, head(heads[m])], v_ref[:, head(heads[m])])

    return call(
        kernel,
        [f32(group, HEAD_DIM, HEAD_DIM)] + [pltpu.VMEM(keys.shape, keys.dtype)] * 2,
        (pltpu.with_memory_space_constraint(keys, pltpu.HBM), pltpu.with_memory_space_constraint(values, pltpu.HBM)),
        2 * group * tokens * HEAD_DIM * HEAD_DIM,
        ins=[HBM, HBM],
        scratch=[pltpu.SemaphoreType.DMA((2, 2))],
    )


def kept_states(keys, values, group):
    tokens = keys.shape[0]

    def kernel(k_ref, v_ref, s_ref):
        for n, h in enumerate(heads_of(lax.axis_index("narrow"), place_in_cube(group), group)):
            s_ref[n] = state(k_ref[:, head(h)], v_ref[:, head(h)])

    return call(
        kernel, f32(group, HEAD_DIM, HEAD_DIM), (keys, values), 2 * group * tokens * HEAD_DIM * HEAD_DIM
    )


def state(k, v):
    return lax.dot_general(k, v, (((0,), (0,)), ((), ())), preferred_element_type=jnp.float32)


def local_part(queries, keys, values):
    tokens = queries.shape[0]

    def kernel(q_ref, k_ref, v_ref, o_ref):
        rows = lax.broadcasted_iota(jnp.int32, (tokens, tokens), 0)
        cols = lax.broadcasted_iota(jnp.int32, (tokens, tokens), 1)
        causal = rows >= cols
        for h in range(HEADS):
            c = slice(h * HEAD_DIM, (h + 1) * HEAD_DIM)
            scores = lax.dot_general(
                q_ref[:, c], k_ref[:, c], (((1,), (1,)), ((), ())), preferred_element_type=jnp.float32
            )
            scores = jnp.where(causal, scores, 0.0).astype(jnp.bfloat16)
            o_ref[:, c] = jnp.dot(scores, v_ref[:, c], preferred_element_type=jnp.float32)

    return call(
        kernel, f32(tokens, HEADS * HEAD_DIM), (queries, keys, values), 4 * HEADS * tokens * tokens * HEAD_DIM
    )


def attended(q, local, carry):
    high = carry.astype(jnp.bfloat16)
    low = (carry - high.astype(jnp.float32)).astype(jnp.bfloat16)
    total = local + jnp.dot(
        jnp.concatenate([q, q], axis=1), jnp.concatenate([high, low], axis=0), preferred_element_type=jnp.float32
    )
    factor = lax.rsqrt(jnp.mean(total * total, axis=-1, keepdims=True) + 1e-05)
    return (total * factor).astype(jnp.bfloat16)


def finish_own(queries, local, pieces, got, group):
    tokens = queries.shape[0]
    turns = turns_of(group)

    def kernel(q_ref, l_ref, g_ref, *refs):
        o_ref = refs[-1]
        core = lax.axis_index("narrow")
        for n, h in enumerate(heads_of(core, place_in_cube(group), group)):
            carry = piece(refs, n, turns) + jnp.where(core == 1, g_ref[n], 0.0)
            o_ref[:, head(h)] = attended(q_ref[:, head(h)], l_ref[:, head(h)], carry)

    return call(
        kernel,
        pltpu.VMEM(queries.shape, jnp.bfloat16),
        (queries, local, got, *pieces),
        4 * group * tokens * HEAD_DIM * HEAD_DIM,
    )


def finish_other(queries, local, carry, done, group, parts=2):
    tokens = queries.shape[0]
    rows = tokens // parts

    def kernel(q_ref, l_ref, c_ref, d_ref, o_hbm, y_ref, sems):
        del d_ref
        core, place = lax.axis_index("narrow"), place_in_cube(group)
        copies = []
        for p in range(parts):
            some = slice(p * rows, (p + 1) * rows)
            for n, h in enumerate(heads_of(1 - core, place, group)):
                y_ref[some, head(h)] = attended(q_ref[some, head(h)], l_ref[some, head(h)], c_ref[n])
            copies.append(pltpu.make_async_copy(y_ref.at[some, :], o_hbm.at[some, :], sems.at[p]))
            copies[-1].start()
        for copy in copies:
            copy.wait()

    return call(
        kernel,
        [jax.ShapeDtypeStruct(queries.shape, jnp.bfloat16), pltpu.VMEM(queries.shape, jnp.bfloat16)],
        (queries, local, carry, done),
        4 * group * tokens * HEAD_DIM * HEAD_DIM,
        out_specs=[HBM, VMEM],
        scratch=[pltpu.SemaphoreType.DMA((parts,))],
        aliases={3: 1},
    )[0]


def piece(refs, n, turns):
    return refs[n // 2][n % 2] if n < 2 * turns else refs[n - turns][...]


def chip_pieces(kept, got):
    group = kept.shape[0]
    turns = turns_of(group)

    def kernel(a_ref, b_ref, *o_refs):
        for turn in range(turns):
            for n in range(2):
                o_refs[turn][n] = a_ref[2 * turn + n] + b_ref[2 * turn + n]
        o_refs[turns][...] = a_ref[group - 2] + b_ref[group - 2]
        o_refs[turns + 1][...] = a_ref[group - 1] + b_ref[group - 1]

    shape = kept.shape[1:]
    return call(kernel, [f32(2, *shape)] * turns + [f32(*shape)] * 2, (kept, got))


def for_other_core(pairs):
    def kernel(*refs):
        other = 1 - lax.axis_index("narrow")
        for n, ref in enumerate(refs[:-1]):
            refs[-1][n] = ref[other]

    return call(kernel, f32(len(pairs), *pairs[0].shape[1:]), pairs)


def ends(core, own, far):
    return jnp.where(core == 0, own, far), jnp.where(core == 0, far, own)


def gathered(pairs, swapped, near, own):
    turns = len(pairs)

    def kernel(*refs):
        pair_refs, (s_ref, far_ref, own_ref, t_ref, p_ref) = refs[:turns], refs[turns:]
        core = lax.axis_index("narrow")
        own, far = own_ref[...], far_ref[...]
        p_ref[turns], p_ref[turns + 1] = ends(core, own, far)
        run = own + far
        for turn in range(turns):
            mine = pair_refs[turn][core]
            p_ref[turn] = mine
            run = run + mine + s_ref[turn]
        t_ref[...] = run

    shape = own.shape
    return call(kernel, [f32(*shape), f32(turns + 2, *shape)], (*pairs, swapped, near, own))


def prefix_at(blocks, corner, k):
    total, sums, bit = 0.0, blocks, 0
    while len(sums) > 1:
        inside = ((corner ^ k) >> bit & 1).astype(jnp.float32)
        total = total + sums[(k >> bit) ^ 1] * inside
        sums = [sums[i] + sums[i + 1] for i in range(0, len(sums), 2)]
        bit += 1
    return total


def cube_prefixes(pairs, swapped, near, own, received, group):
    turns = turns_of(group)
    rows = own.shape[0] // 4

    def kernel(*refs):
        pair_refs, (s_ref, far_ref, own_ref, r_ref) = refs[:turns], refs[turns : turns + 4]
        outs = refs[turns + 4 :]
        core, place = lax.axis_index("narrow"), place_in_cube(group)
        corner = place ^ (NEAR * core)
        for part in range(4):
            some = slice(part * rows, (part + 1) * rows)
            mine, other = [None] * group, [None] * group
            mine[0], mine[NEAR] = ends(core, own_ref[some], far_ref[some])
            other[NEAR], other[0] = r_ref[turns, some], r_ref[turns + 1, some]
            for turn in range(turns):
                mine[partner(0, turn, group)] = pair_refs[turn][core, some]
                mine[NEAR ^ partner(0, turn, group)] = s_ref[turn, some]
                other[partner(0, turn, group)] = pair_refs[turn][1 - core, some]
                other[NEAR ^ partner(0, turn, group)] = r_ref[turn, some]
            for turn in range(turns):
                outs[turn][core, some] = prefix_at(mine, corner, partner(0, turn, group))
                outs[turn][1 - core, some] = prefix_at(other, corner, partner(0, turn, group))
            own_sum, far_sum = ends(core, prefix_at(mine, corner, 0), prefix_at(mine, corner, NEAR))
            outs[turns][some] = far_sum
            outs[turns + 1][some] = own_sum

    shape = own.shape
    return call(
        kernel, [f32(2, *shape)] * turns + [f32(*shape)] * 2, (*pairs, swapped, near, own, received)
    )


def add_earlier(pieces, earlier, others, upper_only, group):
    count = len(pieces)

    def kernel(e_ref, o_ref, *refs):
        core = lax.axis_index("narrow")
        mine, other = e_ref[...], o_ref[...]
        if upper_only:
            upper = lax.axis_index("wide") >= group
            mine, other = jnp.where(upper, mine, 0.0), jnp.where(upper, other, 0.0)
        for ref, out in zip(refs[:count], refs[count:]):
            if len(ref.shape) == 3:
                out[core] = ref[core] + mine
                out[1 - core] = ref[1 - core] + other
            else:
                out[...] = ref[...] + mine

    return call(kernel, [f32(*piece.shape) for piece in pieces], (earlier, others, *pieces))


def add_lower(pieces, kept):
    group = kept.shape[0]
    turns = turns_of(group)

    def kernel(k_ref, *refs):
        lower = lax.axis_index("narrow") == 0
        for n in range(group):
            refs[-1][n] = piece(refs, n, turns) + jnp.where(lower, k_ref[n], 0.0)

    return call(kernel, f32(*kept.shape), (kept, *pieces))


def swap_cores(block):
    return lax.ppermute(block, "narrow", [(0, 1), (1, 0)])


def pair_chips(block, chips, cores, of):
    route = [(i * cores + c, (i ^ of(c)) * cores + c) for i in range(chips) for c in range(cores)]
    return lax.ppermute(block, ("wide", "narrow"), route)


def pairings(pairs, near, chips, cores, group):
    pairs = [
        pair_chips(pair, chips, cores, lambda c, turn=turn: partner(c, turn, group)) for turn, pair in enumerate(pairs)
    ]
    return pairs, pair_chips(near, chips, cores, lambda c: NEAR)


def shards(queries, keys, values):
    chips, cores = lax.axis_size("wide"), lax.axis_size("narrow")
    group = HEADS // cores
    groups = chips // group

    given, keys, values = first_states(keys, values, group)
    got = swap_cores(given)
    kept = kept_states(keys, values, group)
    *pairs, near, mine = chip_pieces(kept, got)
    later_q, _ = lax.optimization_barrier((queries, mine))
    pairs, near = pairings(pairs, near, chips, cores, group)
    local = local_part(later_q, keys, values)
    *pairs, near, local = lax.optimization_barrier((*pairs, near, local))
    swapped = swap_cores(for_other_core(pairs))
    running, lacking = gathered(pairs, swapped, near, mine)
    cube = lax.axis_index("wide") // group
    earlier = jnp.zeros_like(running) if groups != 2 else None
    crossed = 1 if groups == 2 else 0
    step = 1
    while step < groups:
        seen = lax.ppermute(
            running,
            ("wide", "narrow"),
            [(i * cores + c, (i ^ (step * group)) * cores + (c ^ crossed)) for i in range(chips) for c in range(cores)],
        )
        earlier = seen if groups == 2 else earlier + jnp.where((cube & step) != 0, seen, 0.0)
        running = running + seen
        step *= 2
    received = swap_cores(lacking)
    earlier, received = lax.optimization_barrier((earlier, received))
    others = swap_cores(earlier)
    if crossed:
        earlier, others = others, earlier
    pieces = cube_prefixes(pairs, swapped, near, mine, received, group)
    others, *pieces = lax.optimization_barrier((others, *pieces))
    *pairs, far, mine = add_earlier(pieces, earlier, others, groups == 2, group)
    pairs, far = pairings(pairs, far, chips, cores, group)
    pieces = lax.optimization_barrier((*pairs, far, mine))
    other = swap_cores(add_lower(pieces, kept))
    own = finish_own(queries, local, pieces, got, group)
    return finish_other(queries, local, other, own, group)


def solution(mesh):
    placed = P(("wide", "narrow"), None)
    return jax.shard_map(
        shards, mesh=mesh, in_specs=(placed, placed, placed), out_specs=placed, check_vma=False
    )
```

```python
import jax
import jax.numpy as jnp
from jax import lax
from jax.experimental import pallas as pl
from jax.experimental.pallas import tpu as pltpu
from jax.sharding import PartitionSpec as P

HEADS = 16
HEAD_DIM = 128
VMEM = pl.BlockSpec(memory_space=pltpu.VMEM)
HBM = pl.BlockSpec(memory_space=pltpu.HBM)
NEAR = HEADS // 4
LIMIT = 8 * 1024 * 1024


def call(kernel, outs, args, flops=0, ins=None, out_specs=None, scratch=(), aliases={}):
    moved = sum(a.size * a.dtype.itemsize for a in args)
    return pl.pallas_call(
        kernel,
        out_shape=outs,
        in_specs=ins or [VMEM] * len(args),
        out_specs=out_specs or ([VMEM] * len(outs) if isinstance(outs, list) else VMEM),
        scratch_shapes=scratch,
        input_output_aliases=aliases,
        compiler_params=pltpu.CompilerParams(vmem_limit_bytes=LIMIT),
        cost_estimate=pl.CostEstimate(flops=flops, bytes_accessed=moved, transcendentals=0),
    )(*args)


def f32(*shape):
    return pltpu.VMEM(shape, jnp.float32)


def head(h, first=0):
    return pl.ds(pl.multiple_of(first + h * HEAD_DIM, HEAD_DIM), HEAD_DIM)


def place_in_cube(group):
    return lax.rem(lax.axis_index("wide"), group)


def partner(core, turn, group):
    return (turn or group - 1) ^ (NEAR * core)


def turns_of(group):
    return (group - 2) // 2


def heads_of(core, place, group):
    heads = []
    for turn in range(turns_of(group)):
        owner = place ^ partner(core, turn, group)
        heads += [owner, group + owner]
    return heads + [core * group + (place ^ NEAR), core * group + place]


def first_states(keys, values, group):
    tokens, width = keys.shape
    part = width // 2

    def kernel(k_hbm, v_hbm, s_ref, k_ref, v_ref, sems):
        copies = []
        for n in range(2):
            cols = slice(n * part, (n + 1) * part)
            for i, (src, dst) in enumerate(((k_hbm, k_ref), (v_hbm, v_ref))):
                copies.append(pltpu.make_async_copy(src.at[:, cols], dst.at[:, cols], sems.at[n, i]))
                copies[-1].start()
        heads = heads_of(1 - lax.axis_index("narrow"), place_in_cube(group), group)
        lower = [2 * turn for turn in range(turns_of(group))]
        for n in range(2):
            copies[2 * n].wait()
            copies[2 * n + 1].wait()
            for m in lower if n == 0 else [m for m in range(group) if m not in lower]:
                s_ref[m] = state(k_ref[:, head(heads[m])], v_ref[:, head(heads[m])])

    return call(
        kernel,
        [f32(group, HEAD_DIM, HEAD_DIM)] + [pltpu.VMEM(keys.shape, keys.dtype)] * 2,
        (pltpu.with_memory_space_constraint(keys, pltpu.HBM), pltpu.with_memory_space_constraint(values, pltpu.HBM)),
        2 * group * tokens * HEAD_DIM * HEAD_DIM,
        ins=[HBM, HBM],
        scratch=[pltpu.SemaphoreType.DMA((2, 2))],
    )


def kept_states(keys, values, group):
    tokens = keys.shape[0]

    def kernel(k_ref, v_ref, s_ref):
        for n, h in enumerate(heads_of(lax.axis_index("narrow"), place_in_cube(group), group)):
            s_ref[n] = state(k_ref[:, head(h)], v_ref[:, head(h)])

    return call(
        kernel, f32(group, HEAD_DIM, HEAD_DIM), (keys, values), 2 * group * tokens * HEAD_DIM * HEAD_DIM
    )


def state(k, v):
    return lax.dot_general(k, v, (((0,), (0,)), ((), ())), preferred_element_type=jnp.float32)


def local_part(queries, keys, values):
    tokens = queries.shape[0]

    def kernel(q_ref, k_ref, v_ref, o_ref):
        rows = lax.broadcasted_iota(jnp.int32, (tokens, tokens), 0)
        cols = lax.broadcasted_iota(jnp.int32, (tokens, tokens), 1)
        causal = rows >= cols
        for h in range(HEADS):
            c = slice(h * HEAD_DIM, (h + 1) * HEAD_DIM)
            scores = lax.dot_general(
                q_ref[:, c], k_ref[:, c], (((1,), (1,)), ((), ())), preferred_element_type=jnp.float32
            )
            scores = jnp.where(causal, scores, 0.0).astype(jnp.bfloat16)
            o_ref[:, c] = jnp.dot(scores, v_ref[:, c], preferred_element_type=jnp.float32)

    return call(
        kernel, f32(tokens, HEADS * HEAD_DIM), (queries, keys, values), 4 * HEADS * tokens * tokens * HEAD_DIM
    )


def attended(q, local, carry):
    high = carry.astype(jnp.bfloat16)
    low = (carry - high.astype(jnp.float32)).astype(jnp.bfloat16)
    total = local + jnp.dot(
        jnp.concatenate([q, q], axis=1), jnp.concatenate([high, low], axis=0), preferred_element_type=jnp.float32
    )
    factor = lax.rsqrt(jnp.mean(total * total, axis=-1, keepdims=True) + 1e-05)
    return (total * factor).astype(jnp.bfloat16)


def finish_own(queries, local, pieces, got, group):
    tokens = queries.shape[0]
    turns = turns_of(group)

    def kernel(q_ref, l_ref, g_ref, *refs):
        o_ref = refs[-1]
        core = lax.axis_index("narrow")
        for n, h in enumerate(heads_of(core, place_in_cube(group), group)):
            carry = piece(refs, n, turns) + jnp.where(core == 1, g_ref[n], 0.0)
            o_ref[:, head(h)] = attended(q_ref[:, head(h)], l_ref[:, head(h)], carry)

    return call(
        kernel,
        pltpu.VMEM(queries.shape, jnp.bfloat16),
        (queries, local, got, *pieces),
        4 * group * tokens * HEAD_DIM * HEAD_DIM,
    )


def finish_other(queries, local, carry, done, group, parts=2):
    tokens = queries.shape[0]
    rows = tokens // parts

    def kernel(q_ref, l_ref, c_ref, d_ref, o_hbm, y_ref, sems):
        del d_ref
        core, place = lax.axis_index("narrow"), place_in_cube(group)
        copies = []
        for p in range(parts):
            some = slice(p * rows, (p + 1) * rows)
            for n, h in enumerate(heads_of(1 - core, place, group)):
                y_ref[some, head(h)] = attended(q_ref[some, head(h)], l_ref[some, head(h)], c_ref[n])
            copies.append(pltpu.make_async_copy(y_ref.at[some, :], o_hbm.at[some, :], sems.at[p]))
            copies[-1].start()
        for copy in copies:
            copy.wait()

    return call(
        kernel,
        [jax.ShapeDtypeStruct(queries.shape, jnp.bfloat16), pltpu.VMEM(queries.shape, jnp.bfloat16)],
        (queries, local, carry, done),
        4 * group * tokens * HEAD_DIM * HEAD_DIM,
        out_specs=[HBM, VMEM],
        scratch=[pltpu.SemaphoreType.DMA((parts,))],
        aliases={3: 1},
    )[0]


def piece(refs, n, turns):
    return refs[n // 2][n % 2] if n < 2 * turns else refs[n - turns][...]


def chip_pieces(kept, got):
    group = kept.shape[0]
    turns = turns_of(group)

    def kernel(a_ref, b_ref, *o_refs):
        for turn in range(turns):
            for n in range(2):
                o_refs[turn][n] = a_ref[2 * turn + n] + b_ref[2 * turn + n]
        o_refs[turns][...] = a_ref[group - 2] + b_ref[group - 2]
        o_refs[turns + 1][...] = a_ref[group - 1] + b_ref[group - 1]

    shape = kept.shape[1:]
    return call(kernel, [f32(2, *shape)] * turns + [f32(*shape)] * 2, (kept, got))


def for_other_core(pairs):
    def kernel(*refs):
        other = 1 - lax.axis_index("narrow")
        for n, ref in enumerate(refs[:-1]):
            refs[-1][n] = ref[other]

    return call(kernel, f32(len(pairs), *pairs[0].shape[1:]), pairs)


def ends(core, own, far):
    return jnp.where(core == 0, own, far), jnp.where(core == 0, far, own)


def gathered(pairs, swapped, near, own):
    turns = len(pairs)

    def kernel(*refs):
        pair_refs, (s_ref, far_ref, own_ref, t_ref, p_ref) = refs[:turns], refs[turns:]
        core = lax.axis_index("narrow")
        own, far = own_ref[...], far_ref[...]
        p_ref[turns], p_ref[turns + 1] = ends(core, own, far)
        run = own + far
        for turn in range(turns):
            mine = pair_refs[turn][core]
            p_ref[turn] = mine
            run = run + mine + s_ref[turn]
        t_ref[...] = run

    shape = own.shape
    return call(kernel, [f32(*shape), f32(turns + 2, *shape)], (*pairs, swapped, near, own))


def prefix_at(blocks, corner, k):
    total, sums, bit = 0.0, blocks, 0
    while len(sums) > 1:
        inside = ((corner ^ k) >> bit & 1).astype(jnp.float32)
        total = total + sums[(k >> bit) ^ 1] * inside
        sums = [sums[i] + sums[i + 1] for i in range(0, len(sums), 2)]
        bit += 1
    return total


def cube_prefixes(pairs, swapped, near, own, received, group):
    turns = turns_of(group)
    rows = own.shape[0] // 4

    def kernel(*refs):
        pair_refs, (s_ref, far_ref, own_ref, r_ref) = refs[:turns], refs[turns : turns + 4]
        outs = refs[turns + 4 :]
        core, place = lax.axis_index("narrow"), place_in_cube(group)
        corner = place ^ (NEAR * core)
        for part in range(4):
            some = slice(part * rows, (part + 1) * rows)
            mine, other = [None] * group, [None] * group
            mine[0], mine[NEAR] = ends(core, own_ref[some], far_ref[some])
            other[NEAR], other[0] = r_ref[turns, some], r_ref[turns + 1, some]
            for turn in range(turns):
                mine[partner(0, turn, group)] = pair_refs[turn][core, some]
                mine[NEAR ^ partner(0, turn, group)] = s_ref[turn, some]
                other[partner(0, turn, group)] = pair_refs[turn][1 - core, some]
                other[NEAR ^ partner(0, turn, group)] = r_ref[turn, some]
            for turn in range(turns):
                outs[turn][core, some] = prefix_at(mine, corner, partner(0, turn, group))
                outs[turn][1 - core, some] = prefix_at(other, corner, partner(0, turn, group))
            own_sum, far_sum = ends(core, prefix_at(mine, corner, 0), prefix_at(mine, corner, NEAR))
            outs[turns][some] = far_sum
            outs[turns + 1][some] = own_sum

    shape = own.shape
    return call(
        kernel, [f32(2, *shape)] * turns + [f32(*shape)] * 2, (*pairs, swapped, near, own, received)
    )


def add_earlier(pieces, earlier, others, upper_only, group):
    count = len(pieces)

    def kernel(e_ref, o_ref, *refs):
        core = lax.axis_index("narrow")
        mine, other = e_ref[...], o_ref[...]
        if upper_only:
            upper = lax.axis_index("wide") >= group
            mine, other = jnp.where(upper, mine, 0.0), jnp.where(upper, other, 0.0)
        for ref, out in zip(refs[:count], refs[count:]):
            if len(ref.shape) == 3:
                out[core] = ref[core] + mine
                out[1 - core] = ref[1 - core] + other
            else:
                out[...] = ref[...] + mine

    return call(kernel, [f32(*piece.shape) for piece in pieces], (earlier, others, *pieces))


def add_lower(pieces, kept):
    group = kept.shape[0]
    turns = turns_of(group)

    def kernel(k_ref, *refs):
        lower = lax.axis_index("narrow") == 0
        for n in range(group):
            refs[-1][n] = piece(refs, n, turns) + jnp.where(lower, k_ref[n], 0.0)

    return call(kernel, f32(*kept.shape), (kept, *pieces))


def swap_cores(block):
    return lax.ppermute(block, "narrow", [(0, 1), (1, 0)])


def pair_chips(block, chips, cores, of):
    route = [(i * cores + c, (i ^ of(c)) * cores + c) for i in range(chips) for c in range(cores)]
    return lax.ppermute(block, ("wide", "narrow"), route)


def pairings(pairs, near, chips, cores, group):
    pairs = [
        pair_chips(pair, chips, cores, lambda c, turn=turn: partner(c, turn, group)) for turn, pair in enumerate(pairs)
    ]
    return pairs, pair_chips(near, chips, cores, lambda c: NEAR)


def shards(queries, keys, values):
    chips, cores = lax.axis_size("wide"), lax.axis_size("narrow")
    group = HEADS // cores
    groups = chips // group

    given, keys, values = first_states(keys, values, group)
    got = swap_cores(given)
    kept = kept_states(keys, values, group)
    *pairs, near, mine = chip_pieces(kept, got)
    later_q, _ = lax.optimization_barrier((queries, mine))
    pairs, near = pairings(pairs, near, chips, cores, group)
    local = local_part(later_q, keys, values)
    *pairs, near, local = lax.optimization_barrier((*pairs, near, local))
    swapped = swap_cores(for_other_core(pairs))
    running, lacking = gathered(pairs, swapped, near, mine)
    cube = lax.axis_index("wide") // group
    earlier = jnp.zeros_like(running) if groups != 2 else None
    crossed = 1 if groups == 2 else 0
    step = 1
    while step < groups:
        seen = lax.ppermute(
            running,
            ("wide", "narrow"),
            [(i * cores + c, (i ^ (step * group)) * cores + (c ^ crossed)) for i in range(chips) for c in range(cores)],
        )
        earlier = seen if groups == 2 else earlier + jnp.where((cube & step) != 0, seen, 0.0)
        running = running + seen
        step *= 2
    received = swap_cores(lacking)
    earlier, received = lax.optimization_barrier((earlier, received))
    others = swap_cores(earlier)
    if crossed:
        earlier, others = others, earlier
    pieces = cube_prefixes(pairs, swapped, near, mine, received, group)
    others, *pieces = lax.optimization_barrier((others, *pieces))
    *pairs, far, mine = add_earlier(pieces, earlier, others, groups == 2, group)
    pairs, far = pairings(pairs, far, chips, cores, group)
    pieces = lax.optimization_barrier((*pairs, far, mine))
    other = swap_cores(add_lower(pieces, kept))
    own = finish_own(queries, local, pieces, got, group)
    return finish_other(queries, local, other, own, group)


def solution(mesh):
    placed = P(("wide", "narrow"), None)
    return jax.shard_map(
        shards, mesh=mesh, in_specs=(placed, placed, placed), out_specs=placed, check_vma=False
    )
```

```python
import jax
import jax.numpy as jnp
from jax import lax
from jax.experimental import pallas as pl
from jax.experimental.pallas import tpu as pltpu
from jax.sharding import PartitionSpec as P

HEADS = 16
HEAD_DIM = 128
VMEM = pl.BlockSpec(memory_space=pltpu.VMEM)
HBM = pl.BlockSpec(memory_space=pltpu.HBM)
NEAR = HEADS // 4
LIMIT = 8 * 1024 * 1024


def call(kernel, outs, args, flops=0, ins=None, out_specs=None, scratch=(), aliases={}):
    moved = sum(a.size * a.dtype.itemsize for a in args)
    return pl.pallas_call(
        kernel,
        out_shape=outs,
        in_specs=ins or [VMEM] * len(args),
        out_specs=out_specs or ([VMEM] * len(outs) if isinstance(outs, list) else VMEM),
        scratch_shapes=scratch,
        input_output_aliases=aliases,
        compiler_params=pltpu.CompilerParams(vmem_limit_bytes=LIMIT),
        cost_estimate=pl.CostEstimate(flops=flops, bytes_accessed=moved, transcendentals=0),
    )(*args)


def f32(*shape):
    return pltpu.VMEM(shape, jnp.float32)


def head(h, first=0):
    return pl.ds(pl.multiple_of(first + h * HEAD_DIM, HEAD_DIM), HEAD_DIM)


def place_in_cube(group):
    return lax.rem(lax.axis_index("wide"), group)


def partner(core, turn, group):
    return (turn or group - 1) ^ (NEAR * core)


def turns_of(group):
    return (group - 2) // 2


def heads_of(core, place, group):
    heads = []
    for turn in range(turns_of(group)):
        owner = place ^ partner(core, turn, group)
        heads += [owner, group + owner]
    return heads + [core * group + (place ^ NEAR), core * group + place]


def first_states(keys, values, group):
    tokens, width = keys.shape
    part = width // 2

    def kernel(k_hbm, v_hbm, s_ref, k_ref, v_ref, sems):
        copies = []
        for n in range(2):
            cols = slice(n * part, (n + 1) * part)
            for i, (src, dst) in enumerate(((k_hbm, k_ref), (v_hbm, v_ref))):
                copies.append(pltpu.make_async_copy(src.at[:, cols], dst.at[:, cols], sems.at[n, i]))
                copies[-1].start()
        heads = heads_of(1 - lax.axis_index("narrow"), place_in_cube(group), group)
        lower = [2 * turn for turn in range(turns_of(group))]
        for n in range(2):
            copies[2 * n].wait()
            copies[2 * n + 1].wait()
            for m in lower if n == 0 else [m for m in range(group) if m not in lower]:
                s_ref[m] = state(k_ref[:, head(heads[m])], v_ref[:, head(heads[m])])

    return call(
        kernel,
        [f32(group, HEAD_DIM, HEAD_DIM)] + [pltpu.VMEM(keys.shape, keys.dtype)] * 2,
        (pltpu.with_memory_space_constraint(keys, pltpu.HBM), pltpu.with_memory_space_constraint(values, pltpu.HBM)),
        2 * group * tokens * HEAD_DIM * HEAD_DIM,
        ins=[HBM, HBM],
        scratch=[pltpu.SemaphoreType.DMA((2, 2))],
    )


def kept_states(keys, values, group):
    tokens = keys.shape[0]

    def kernel(k_ref, v_ref, s_ref):
        for n, h in enumerate(heads_of(lax.axis_index("narrow"), place_in_cube(group), group)):
            s_ref[n] = state(k_ref[:, head(h)], v_ref[:, head(h)])

    return call(
        kernel, f32(group, HEAD_DIM, HEAD_DIM), (keys, values), 2 * group * tokens * HEAD_DIM * HEAD_DIM
    )


def state(k, v):
    return lax.dot_general(k, v, (((0,), (0,)), ((), ())), preferred_element_type=jnp.float32)


def local_part(queries, keys, values):
    tokens = queries.shape[0]

    def kernel(q_ref, k_ref, v_ref, o_ref):
        rows = lax.broadcasted_iota(jnp.int32, (tokens, tokens), 0)
        cols = lax.broadcasted_iota(jnp.int32, (tokens, tokens), 1)
        causal = rows >= cols
        for h in range(HEADS):
            c = slice(h * HEAD_DIM, (h + 1) * HEAD_DIM)
            scores = lax.dot_general(
                q_ref[:, c], k_ref[:, c], (((1,), (1,)), ((), ())), preferred_element_type=jnp.float32
            )
            scores = jnp.where(causal, scores, 0.0).astype(jnp.bfloat16)
            o_ref[:, c] = jnp.dot(scores, v_ref[:, c], preferred_element_type=jnp.float32)

    return call(
        kernel, f32(tokens, HEADS * HEAD_DIM), (queries, keys, values), 4 * HEADS * tokens * tokens * HEAD_DIM
    )


def attended(q, local, carry):
    high = carry.astype(jnp.bfloat16)
    low = (carry - high.astype(jnp.float32)).astype(jnp.bfloat16)
    total = local + jnp.dot(
        jnp.concatenate([q, q], axis=1), jnp.concatenate([high, low], axis=0), preferred_element_type=jnp.float32
    )
    factor = lax.rsqrt(jnp.mean(total * total, axis=-1, keepdims=True) + 1e-05)
    return (total * factor).astype(jnp.bfloat16)


def finish_own(queries, local, pieces, got, group):
    tokens = queries.shape[0]
    turns = turns_of(group)

    def kernel(q_ref, l_ref, g_ref, *refs):
        o_ref = refs[-1]
        core = lax.axis_index("narrow")
        for n, h in enumerate(heads_of(core, place_in_cube(group), group)):
            carry = piece(refs, n, turns) + jnp.where(core == 1, g_ref[n], 0.0)
            o_ref[:, head(h)] = attended(q_ref[:, head(h)], l_ref[:, head(h)], carry)

    return call(
        kernel,
        pltpu.VMEM(queries.shape, jnp.bfloat16),
        (queries, local, got, *pieces),
        4 * group * tokens * HEAD_DIM * HEAD_DIM,
    )


def finish_other(queries, local, carry, done, group, parts=2):
    tokens = queries.shape[0]
    rows = tokens // parts

    def kernel(q_ref, l_ref, c_ref, d_ref, o_hbm, y_ref, sems):
        del d_ref
        core, place = lax.axis_index("narrow"), place_in_cube(group)
        copies = []
        for p in range(parts):
            some = slice(p * rows, (p + 1) * rows)
            for n, h in enumerate(heads_of(1 - core, place, group)):
                y_ref[some, head(h)] = attended(q_ref[some, head(h)], l_ref[some, head(h)], c_ref[n])
            copies.append(pltpu.make_async_copy(y_ref.at[some, :], o_hbm.at[some, :], sems.at[p]))
            copies[-1].start()
        for copy in copies:
            copy.wait()

    return call(
        kernel,
        [jax.ShapeDtypeStruct(queries.shape, jnp.bfloat16), pltpu.VMEM(queries.shape, jnp.bfloat16)],
        (queries, local, carry, done),
        4 * group * tokens * HEAD_DIM * HEAD_DIM,
        out_specs=[HBM, VMEM],
        scratch=[pltpu.SemaphoreType.DMA((parts,))],
        aliases={3: 1},
    )[0]


def piece(refs, n, turns):
    return refs[n // 2][n % 2] if n < 2 * turns else refs[n - turns][...]


def chip_pieces(kept, got):
    group = kept.shape[0]
    turns = turns_of(group)

    def kernel(a_ref, b_ref, *o_refs):
        for turn in range(turns):
            for n in range(2):
                o_refs[turn][n] = a_ref[2 * turn + n] + b_ref[2 * turn + n]
        o_refs[turns][...] = a_ref[group - 2] + b_ref[group - 2]
        o_refs[turns + 1][...] = a_ref[group - 1] + b_ref[group - 1]

    shape = kept.shape[1:]
    return call(kernel, [f32(2, *shape)] * turns + [f32(*shape)] * 2, (kept, got))


def for_other_core(pairs):
    def kernel(*refs):
        other = 1 - lax.axis_index("narrow")
        for n, ref in enumerate(refs[:-1]):
            refs[-1][n] = ref[other]

    return call(kernel, f32(len(pairs), *pairs[0].shape[1:]), pairs)


def ends(core, own, far):
    return jnp.where(core == 0, own, far), jnp.where(core == 0, far, own)


def gathered(pairs, swapped, near, own):
    turns = len(pairs)

    def kernel(*refs):
        pair_refs, (s_ref, far_ref, own_ref, t_ref, p_ref) = refs[:turns], refs[turns:]
        core = lax.axis_index("narrow")
        own, far = own_ref[...], far_ref[...]
        p_ref[turns], p_ref[turns + 1] = ends(core, own, far)
        run = own + far
        for turn in range(turns):
            mine = pair_refs[turn][core]
            p_ref[turn] = mine
            run = run + mine + s_ref[turn]
        t_ref[...] = run

    shape = own.shape
    return call(kernel, [f32(*shape), f32(turns + 2, *shape)], (*pairs, swapped, near, own))


def prefix_at(blocks, corner, k):
    total, sums, bit = 0.0, blocks, 0
    while len(sums) > 1:
        inside = ((corner ^ k) >> bit & 1).astype(jnp.float32)
        total = total + sums[(k >> bit) ^ 1] * inside
        sums = [sums[i] + sums[i + 1] for i in range(0, len(sums), 2)]
        bit += 1
    return total


def cube_prefixes(pairs, swapped, near, own, received, group):
    turns = turns_of(group)
    rows = own.shape[0] // 4

    def kernel(*refs):
        pair_refs, (s_ref, far_ref, own_ref, r_ref) = refs[:turns], refs[turns : turns + 4]
        outs = refs[turns + 4 :]
        core, place = lax.axis_index("narrow"), place_in_cube(group)
        corner = place ^ (NEAR * core)
        for part in range(4):
            some = slice(part * rows, (part + 1) * rows)
            mine, other = [None] * group, [None] * group
            mine[0], mine[NEAR] = ends(core, own_ref[some], far_ref[some])
            other[NEAR], other[0] = r_ref[turns, some], r_ref[turns + 1, some]
            for turn in range(turns):
                mine[partner(0, turn, group)] = pair_refs[turn][core, some]
                mine[NEAR ^ partner(0, turn, group)] = s_ref[turn, some]
                other[partner(0, turn, group)] = pair_refs[turn][1 - core, some]
                other[NEAR ^ partner(0, turn, group)] = r_ref[turn, some]
            for turn in range(turns):
                outs[turn][core, some] = prefix_at(mine, corner, partner(0, turn, group))
                outs[turn][1 - core, some] = prefix_at(other, corner, partner(0, turn, group))
            own_sum, far_sum = ends(core, prefix_at(mine, corner, 0), prefix_at(mine, corner, NEAR))
            outs[turns][some] = far_sum
            outs[turns + 1][some] = own_sum

    shape = own.shape
    return call(
        kernel, [f32(2, *shape)] * turns + [f32(*shape)] * 2, (*pairs, swapped, near, own, received)
    )


def add_earlier(pieces, earlier, others, upper_only, group):
    count = len(pieces)

    def kernel(e_ref, o_ref, *refs):
        core = lax.axis_index("narrow")
        mine, other = e_ref[...], o_ref[...]
        if upper_only:
            upper = lax.axis_index("wide") >= group
            mine, other = jnp.where(upper, mine, 0.0), jnp.where(upper, other, 0.0)
        for ref, out in zip(refs[:count], refs[count:]):
            if len(ref.shape) == 3:
                out[core] = ref[core] + mine
                out[1 - core] = ref[1 - core] + other
            else:
                out[...] = ref[...] + mine

    return call(kernel, [f32(*piece.shape) for piece in pieces], (earlier, others, *pieces))


def add_lower(pieces, kept):
    group = kept.shape[0]
    turns = turns_of(group)

    def kernel(k_ref, *refs):
        lower = lax.axis_index("narrow") == 0
        for n in range(group):
            refs[-1][n] = piece(refs, n, turns) + jnp.where(lower, k_ref[n], 0.0)

    return call(kernel, f32(*kept.shape), (kept, *pieces))


def swap_cores(block):
    return lax.ppermute(block, "narrow", [(0, 1), (1, 0)])


def pair_chips(block, chips, cores, of):
    route = [(i * cores + c, (i ^ of(c)) * cores + c) for i in range(chips) for c in range(cores)]
    return lax.ppermute(block, ("wide", "narrow"), route)


def pairings(pairs, near, chips, cores, group):
    pairs = [
        pair_chips(pair, chips, cores, lambda c, turn=turn: partner(c, turn, group)) for turn, pair in enumerate(pairs)
    ]
    return pairs, pair_chips(near, chips, cores, lambda c: NEAR)


def shards(queries, keys, values):
    chips, cores = lax.axis_size("wide"), lax.axis_size("narrow")
    group = HEADS // cores
    groups = chips // group

    given, keys, values = first_states(keys, values, group)
    got = swap_cores(given)
    kept = kept_states(keys, values, group)
    *pairs, near, mine = chip_pieces(kept, got)
    pairs, near = pairings(pairs, near, chips, cores, group)
    *pairs, near = lax.optimization_barrier((*pairs, near))
    swapped = swap_cores(for_other_core(pairs))
    running, lacking = gathered(pairs, swapped, near, mine)
    later_q, _ = lax.optimization_barrier((queries, running))
    local = local_part(later_q, keys, values)
    cube = lax.axis_index("wide") // group
    earlier = jnp.zeros_like(running) if groups != 2 else None
    crossed = 1 if groups == 2 else 0
    step = 1
    while step < groups:
        seen = lax.ppermute(
            running,
            ("wide", "narrow"),
            [(i * cores + c, (i ^ (step * group)) * cores + (c ^ crossed)) for i in range(chips) for c in range(cores)],
        )
        earlier = seen if groups == 2 else earlier + jnp.where((cube & step) != 0, seen, 0.0)
        running = running + seen
        step *= 2
    received = swap_cores(lacking)
    earlier, received, local = lax.optimization_barrier((earlier, received, local))
    others = swap_cores(earlier)
    if crossed:
        earlier, others = others, earlier
    pieces = cube_prefixes(pairs, swapped, near, mine, received, group)
    others, *pieces = lax.optimization_barrier((others, *pieces))
    *pairs, far, mine = add_earlier(pieces, earlier, others, groups == 2, group)
    pairs, far = pairings(pairs, far, chips, cores, group)
    pieces = lax.optimization_barrier((*pairs, far, mine))
    other = swap_cores(add_lower(pieces, kept))
    own = finish_own(queries, local, pieces, got, group)
    return finish_other(queries, local, other, own, group)


def solution(mesh):
    placed = P(("wide", "narrow"), None)
    return jax.shard_map(
        shards, mesh=mesh, in_specs=(placed, placed, placed), out_specs=placed, check_vma=False
    )
```
